32 devices in a mesh: dp: 8 (over y, x, core), neg: 4 (over z).
Axes of the slice: x: 2, y: 2, z: 4, core: 2. Of those that a mesh axis runs over, the one named last changes fastest.
Arguments:
- img_features: bfloat16 [64, 256, 1024], P(('dp', 'neg'))
- txt_features: bfloat16 [64, 64, 1024], P(('dp', 'neg'))
- w_img: bfloat16 [1024, 256], replicated
- w_txt: bfloat16 [1024, 256], replicated
- cap_len: int32 [64], P(('dp', 'neg')), may hold values from 16 to 64
- pairs: int32 [8, 8], P('dp'), may hold values from 0 to 7, each once within a row
Outputs:
- grad_img_features: bfloat16 [64, 256, 1024], P(('dp', 'neg'))
- grad_txt_features: bfloat16 [64, 64, 1024], P(('dp', 'neg'))
- grad_w_img: float32 [1024, 256], P('dp')
- grad_w_txt: float32 [1024, 256], P('dp')
The draws below stay inside these ranges and needn't reach their ends.
Inputs may be any that keep to these rules, and one draw needn't show every extreme that they name: `pairs`: each row is a permutation of 0 to 7.
All inputs are finite; a program needn't handle non-finite values.
Results may differ from the reference program's by a relative error of at most 0.011.
Values may be sent and summed in bfloat16 or wider, within the bound.
A program may use at most 64 MiB of HBM per device.

```python
import jax
import jax.numpy as jnp
from jax import lax

D_IN = 1024
EMB = 256
PI = 256
PT = 64
GROUP = 8
IMAGES = 64
N_DP = 8


def shared_weight(key):
    return jax.random.normal(jax.random.fold_in(key, 11), (D_IN, EMB), jnp.float32) * D_IN ** (-0.5)


def group_common(key):
    common = jax.random.normal(jax.random.fold_in(key, 31), (N_DP, 1, 1, D_IN), jnp.float32)
    return jnp.broadcast_to(common, (N_DP, GROUP, 1, D_IN)).reshape(IMAGES, 1, D_IN)


def image_tokens(key, ramp):
    base = jax.random.normal(jax.random.fold_in(key, 21), (IMAGES, PI, D_IN), jnp.float32)
    place = (jnp.arange(IMAGES, dtype=jnp.int32) % GROUP).astype(jnp.float32)
    rising = ramp * place / max(GROUP - 1, 1)
    return base + rising[:, None, None] * group_common(key)


def draw_w_img(key, part):
    return shared_weight(key).astype(jnp.bfloat16)


def draw_w_txt(key, part):
    return (jax.random.normal(jax.random.fold_in(key, 12), (D_IN, EMB), jnp.float32) * D_IN ** (-0.5)).astype(jnp.bfloat16)


def draw_img_features(key, part):
    return image_tokens(key, 0.2).astype(jnp.bfloat16)


def draw_txt_features(key, part):
    common = group_common(key)
    fresh = jax.random.normal(jax.random.fold_in(key, 22), (IMAGES, PT, D_IN), jnp.float32)
    return (fresh + 0.3 * common).astype(jnp.bfloat16)


def touch_ends(drawn, own_key, smallest, high):
    spot = [jax.random.randint(jax.random.fold_in(own_key, axis), (), 0, length) for axis, length in enumerate(drawn.shape)]
    widest = drawn.shape.index(max(drawn.shape))
    next_to = spot[:widest] + [(spot[widest] + 1) % drawn.shape[widest]] + spot[widest + 1:]
    return drawn.at[tuple(spot)].set(smallest).at[tuple(next_to)].set(high)


def setup_inputs(seed: int = 0) -> dict:
    key_of = jax.random.split(jax.random.key(seed), 7)
    img_features = draw_img_features(jax.random.fold_in(key_of[6], 71), 0)
    txt_features = draw_txt_features(jax.random.fold_in(key_of[6], 71), 0)
    w_img = draw_w_img(jax.random.fold_in(key_of[6], 71), 0)
    w_txt = draw_w_txt(jax.random.fold_in(key_of[6], 71), 0)
    cap_len = touch_ends(jax.random.randint(key_of[4], (IMAGES,), PT // 4, PT + 1), jax.random.fold_in(key_of[4], 1), PT // 4, PT).astype(jnp.int32)
    pairs = jax.vmap(lambda own: jax.random.permutation(own, GROUP))(jax.random.split(key_of[5], N_DP)).reshape((N_DP, GROUP)).astype(jnp.int32)
    return {"img_features": img_features, "txt_features": txt_features, "w_img": w_img, "w_txt": w_txt, "cap_len": cap_len, "pairs": pairs}


TOKEN_SCALE = 100.0
PAIR_SCALE = 50.0
EPSILON = 1e-06

def unit_rows(projected):
    inverse = lax.rsqrt(lax.optimization_barrier(jnp.sum(projected * projected, axis=-1, keepdims=True)) + EPSILON)
    return (projected * inverse, inverse)

def back_unit(gradient, unit, inverse):
    return (gradient - unit * lax.optimization_barrier(jnp.sum(unit * gradient, axis=-1, keepdims=True))) * inverse

def token_pool(scores, lengths, count_caps, text_len):
    rows = scores.shape[0]
    logits = (TOKEN_SCALE * scores).reshape(rows, count_caps, text_len)
    valid = (jnp.arange(text_len, dtype=jnp.int32)[None, :] < lengths[:, None])[None]
    peaks = lax.optimization_barrier(jnp.max(jnp.where(valid, logits, -jnp.inf), axis=2, keepdims=True))
    expos = jnp.where(valid, jnp.exp(logits - peaks), 0.0)
    totals = lax.optimization_barrier(jnp.sum(expos, axis=2, keepdims=True))
    pooled = (peaks[..., 0] + jnp.log(totals[..., 0])) / TOKEN_SCALE
    return (pooled, expos / totals)

def group_grads(img, txt, lengths, perm, w_img, w_txt):
    count = img.shape[0]
    img_len = img.shape[1]
    text_len = txt.shape[1]
    img_flat = img.reshape(count * img_len, img.shape[2])
    txt_flat = txt.reshape(count * text_len, txt.shape[2])
    img_unit, img_inv = unit_rows(jnp.dot(img_flat, w_img, preferred_element_type=jnp.float32))
    txt_unit, txt_inv = unit_rows(jnp.dot(txt_flat, w_txt, preferred_element_type=jnp.float32))
    img_half = img_unit.astype(jnp.bfloat16)
    txt_half = txt_unit.astype(jnp.bfloat16)
    scores = jnp.dot(img_half, txt_half.T, preferred_element_type=jnp.float32)
    pooled, weights = token_pool(scores, lengths, count, text_len)
    logits = PAIR_SCALE * lax.optimization_barrier(jnp.mean(pooled.reshape(count, img_len, count), axis=1))
    target = (perm[:, None] == jnp.arange(count, dtype=jnp.int32)[None, :]).astype(jnp.float32)
    row_prob = jax.nn.softmax(logits, axis=1)
    col_prob = jax.nn.softmax(logits, axis=0)
    pair_grad = (row_prob + col_prob - 2.0 * target) * (PAIR_SCALE / (2.0 * count * img_len))
    spread = jnp.broadcast_to(pair_grad[:, None, :], (count, img_len, count)).reshape(count * img_len, count, 1)
    score_grad = (spread * weights).reshape(count * img_len, count * text_len).astype(jnp.bfloat16)
    img_grad = jnp.dot(score_grad, txt_half, preferred_element_type=jnp.float32)
    txt_grad = jnp.dot(score_grad.T, img_half, preferred_element_type=jnp.float32)
    img_back = back_unit(img_grad, img_unit, img_inv).astype(jnp.bfloat16)
    txt_back = back_unit(txt_grad, txt_unit, txt_inv).astype(jnp.bfloat16)
    feat_img = jnp.dot(img_back, w_img.T, preferred_element_type=jnp.float32).astype(jnp.bfloat16)
    feat_txt = jnp.dot(txt_back, w_txt.T, preferred_element_type=jnp.float32).astype(jnp.bfloat16)
    wgrad_img = jnp.dot(img_flat.T, img_back, preferred_element_type=jnp.float32)
    wgrad_txt = jnp.dot(txt_flat.T, txt_back, preferred_element_type=jnp.float32)
    return (feat_img.reshape(img.shape), feat_txt.reshape(txt.shape), wgrad_img, wgrad_txt)

def reference(img_features, txt_features, w_img, w_txt, cap_len, pairs):
    img_groups = img_features.reshape(N_DP, GROUP, PI, D_IN)
    txt_groups = txt_features.reshape(N_DP, GROUP, PT, D_IN)
    len_groups = cap_len.reshape(N_DP, GROUP)

    def one_group(packed):
        return group_grads(packed[0], packed[1], packed[2], packed[3], w_img, w_txt)
    feat_img, feat_txt, wgrad_img, wgrad_txt = lax.map(one_group, (img_groups, txt_groups, len_groups, pairs))
    return (feat_img.reshape(IMAGES, PI, D_IN), feat_txt.reshape(IMAGES, PT, D_IN), lax.optimization_barrier(jnp.sum(wgrad_img, axis=0)), lax.optimization_barrier(jnp.sum(wgrad_txt, axis=0)))
```

```python
import functools

import jax
import jax.numpy as jnp
from jax import lax
from jax.experimental import pallas as pl
from jax.experimental.pallas import tpu as pltpu
from jax.sharding import PartitionSpec as P

TOKEN_SCALE = 100.0
PAIR_SCALE = 50.0
EPSILON = 1e-06
MARK = 4.0
LOW = -1e30
BF = jnp.bfloat16
F32 = jnp.float32
MESH = pl.DeviceIdType.MESH


def nn(a, b):
    return lax.dot_general(a, b, (((1,), (0,)), ((), ())), preferred_element_type=F32)


def nt(a, b):
    return lax.dot_general(a, b, (((1,), (1,)), ((), ())), preferred_element_type=F32)


def unit_rows(projected):
    inverse = lax.rsqrt(jnp.sum(projected * projected, axis=-1, keepdims=True) + EPSILON)
    return projected * inverse, inverse


def back_unit(gradient, unit, inverse):
    return (gradient - unit * jnp.sum(unit * gradient, axis=-1, keepdims=True)) * inverse


class Exchange:
    def __init__(self, me, n, device, slots, send, recv):
        self.me, self.n, self.device = me, n, device
        self.slots, self.send, self.recv = slots, send, recv
        self.started = []

    def peer(self, offset):
        return lax.rem(self.me + offset, self.n)

    def start(self, offset, source):
        copy = pltpu.make_async_remote_copy(
            src_ref=source,
            dst_ref=self.slots.at[self.me],
            send_sem=self.send.at[offset],
            recv_sem=self.recv.at[self.me],
            device_id=self.device(self.peer(offset)),
            device_id_type=MESH,
        )
        copy.start()
        self.started.append(copy)

    def take(self, offset):
        other = self.peer(offset)
        pltpu.make_async_remote_copy(
            src_ref=self.slots.at[other],
            dst_ref=self.slots.at[other],
            send_sem=self.send.at[offset],
            recv_sem=self.recv.at[other],
            device_id=self.device(other),
            device_id_type=MESH,
        ).wait_recv()
        return other

    def finish(self):
        for copy in self.started:
            copy.wait_send()


def kernel(
    dims,
    img_hbm, txt_hbm, wi_hbm, wt_hbm, cap, pairs,
    fi_hbm, ft_hbm, gi_out, gt_out,
    img, txt, wi, wt, img_t, txt_t,
    img_unit, img_inv, img_half, txt_unit, txt_inv,
    text_all, expo, total, logit_all, sg, terms, own_term, term_in,
    img_back, txt_back, wg, core_out, core_in, plane_out, plane_own, plane_in,
    part, part_out, ring_in, full, fi, ft,
    load_sem, save_sem,
    text_s, text_r, logit_s, logit_r, term_s, term_r,
    core_s, core_r, plane_s, plane_r, ring_s, ring_r, full_s, full_r,
):
    L, PI, T, D, W, N, NDP = dims
    H = NDP // 2
    r = D // NDP
    rows_i, rows_t = L * PI, L * T
    dp = lax.axis_index("dp")
    me = lax.axis_index("neg")
    core = lax.rem(dp, 2)
    chip = lax.div(dp, 2)
    split = r % (16 * N) == 0
    rr = r // N if split else r

    loads = [
        pltpu.make_async_copy(source, target, load_sem.at[i])
        for i, (source, target) in enumerate(
            ((txt_hbm, txt), (wt_hbm, wt), (wi_hbm, wi), (img_hbm, img))
        )
    ]
    for load in loads:
        load.start()

    def on_neg(k):
        return (dp, k)

    def on_plane(k):
        return (k * 2 + core, me)

    barrier = pltpu.get_barrier_semaphore()
    for o in range(1, N):
        pl.semaphore_signal(barrier, inc=1, device_id=on_neg(lax.rem(me + o, N)), device_id_type=MESH)
    for o in range(1, H):
        pl.semaphore_signal(
            barrier, inc=1, device_id=on_plane(lax.rem(chip + o, H)), device_id_type=MESH
        )
    mate = (chip * 2 + 1 - core, me)
    pl.semaphore_signal(barrier, inc=1, device_id=mate, device_id_type=MESH)

    loads[0].wait()
    loads[1].wait()
    unit, inverse = unit_rows(nn(txt[...], wt[...]))
    txt_unit[...] = unit
    txt_inv[...] = inverse
    place = lax.broadcasted_iota(jnp.int32, (T, W), 0)
    for c in range(L):
        text_all[me, c * T:(c + 1) * T, :] = jnp.where(
            place < cap[c], unit[c * T:(c + 1) * T], MARK
        ).astype(BF)
    pl.semaphore_wait(barrier, N - 1 + H - 1 + 1)
    text_x = Exchange(me, N, on_neg, text_all, text_s, text_r)
    for o in range(1, N):
        text_x.start(o, text_all.at[me])

    loads[2].wait()
    loads[3].wait()
    for i in range(L):
        rows = slice(i * PI, (i + 1) * PI)
        unit, inverse = unit_rows(nn(img[rows, :], wi[...]))
        img_unit[rows, :] = unit
        img_inv[rows, :] = inverse
        img_half[rows, :] = unit.astype(BF)

    def transpose_features():
        for d in range(0, D, 256):
            for i in range(L):
                img_t[d:d + 256, i * PI:(i + 1) * PI] = img[i * PI:(i + 1) * PI, d:d + 256].T
            txt_t[d:d + 256, :] = txt[:, d:d + 256].T

    lane = lax.broadcasted_iota(jnp.int32, (8, 128), 1)
    line = lax.broadcasted_iota(jnp.int32, (8, 128), 0)

    def pool(j):
        text = text_all[j]
        marks = text[:, 0:128].astype(F32)
        marks = jnp.concatenate([marks] * (rows_i // 128), axis=1)
        scores = jnp.where(marks < 2.0, TOKEN_SCALE * nt(text, img_half[...]), LOW)
        scores = scores.reshape(L, T, rows_i)
        peaks = jnp.max(scores, axis=1, keepdims=True)
        expos = jnp.exp(scores - peaks)
        totals = jnp.sum(expos, axis=1)
        expo[j] = expos.reshape(rows_t, rows_i)
        total[j] = jnp.concatenate([totals, jnp.ones((8 - L, rows_i), F32)], axis=0)
        pooled = peaks[:, 0, :] + jnp.log(totals)
        pooled = jnp.concatenate([pooled, jnp.zeros((8 - L, rows_i), F32)], axis=0)
        tile = jnp.full((8, 128), LOW, F32)
        for i in range(L):
            mean = jnp.sum(pooled[:, i * PI:(i + 1) * PI], axis=1, keepdims=True)
            mean = mean * (PAIR_SCALE / (TOKEN_SCALE * PI))
            tile = jnp.where((lane == i) & (line < L), mean, tile)
        logit_all[me, j] = tile

    pool(me)
    transpose_features()
    for o in range(1, N):
        pool(text_x.take(o))
    logit_x = Exchange(me, N, on_neg, logit_all, logit_s, logit_r)
    for o in range(1, N):
        logit_x.start(o, logit_all.at[me])
    own = logit_all[me]
    row_top = jnp.max(jnp.max(own, axis=0), axis=0, keepdims=True)
    row_exp = jnp.exp(own - row_top[None])
    row_prob = row_exp / jnp.sum(jnp.sum(row_exp, axis=0), axis=0, keepdims=True)[None]
    caption = lax.broadcasted_iota(jnp.int32, (N, 8, 128), 0) * L + lax.broadcasted_iota(
        jnp.int32, (N, 8, 128), 1
    )
    lanes = lax.broadcasted_iota(jnp.int32, (N, 8, 128), 2)
    target = jnp.zeros((N, 8, 128), F32)
    for i in range(L):
        target = jnp.where((lanes == i) & (caption == pairs[0, me * L + i]), 1.0, target)
    for o in range(1, N):
        logit_x.take(o)
    everyone = logit_all[...]
    col_top = jnp.max(jnp.max(everyone, axis=0), axis=-1, keepdims=True)
    col_sum = jnp.sum(
        jnp.sum(jnp.exp(everyone - col_top[None]), axis=0), axis=-1, keepdims=True
    )
    col_prob = jnp.exp(own - col_top) / col_sum
    pair_grad = (row_prob + col_prob - 2.0 * target) * (PAIR_SCALE / (2.0 * N * L * PI))
    own_logits = logit_all.at[me]
    logit_x.finish()
    own_logits[...] = pair_grad

    term_x = Exchange(me, N, on_neg, term_in, term_s, term_r)
    for o in list(range(1, N)) + [0]:
        j = lax.rem(me + o, N)
        pair = own_logits[j]
        spread = jnp.concatenate(
            [jnp.broadcast_to(pair[:, i:i + 1], (8, PI)) for i in range(L)], axis=1
        )
        factor = spread / total[j]
        shares = []
        for c in range(L):
            shares.append((expo[j, c * T:(c + 1) * T, :] * factor[c:c + 1, :]).astype(BF))
        share = jnp.concatenate(shares, axis=0)
        sg[j] = share
        term = nn(share, img_half[...])
        if o == 0:
            own_term[...] = term
        else:
            terms[o] = term.astype(BF)
            term_x.start(o, terms.at[o])

    texts = text_all[...].reshape(N * rows_t, W)
    for i in range(L):
        rows = slice(i * PI, (i + 1) * PI)
        grad = nn(sg[:, :, rows].reshape(N * rows_t, PI).T, texts)
        img_back[rows, :] = back_unit(grad, img_unit[rows, :], img_inv[rows, :]).astype(BF)

    cores = []

    def core_copy(m):
        return pltpu.make_async_remote_copy(
            src_ref=core_out.at[m],
            dst_ref=core_in.at[m],
            send_sem=core_s.at[m],
            recv_sem=core_r.at[m],
            device_id=mate,
            device_id_type=MESH,
        )

    def weight_grad(m, features_t, back):
        step = max(256, r)
        for d in range(0, D, step):
            out = nn(features_t[d:d + step, :], back[...])
            for k in range(d // r, (d + step) // r):
                wg[m, k % 2, k // 2] = out[k * r - d:(k + 1) * r - d]
        core_out[m] = wg[m, 1 - core].astype(BF)
        copy = core_copy(m)
        copy.start()
        cores.append(copy)

    planes = [
        Exchange(chip, H, on_plane, plane_in.at[m], plane_s.at[m], plane_r.at[m]) for m in range(2)
    ]
    rings = [Exchange(me, N, on_neg, ring_in.at[m], ring_s.at[m], ring_r.at[m]) for m in range(2)]
    fulls = [Exchange(me, N, on_neg, full.at[m], full_s.at[m], full_r.at[m]) for m in range(2)]

    def plane_send(m):
        cores[m].wait_recv()
        for o in range(1, H):
            k = planes[m].peer(o)
            plane_out[m, o] = (wg[m, core, k] + core_in[m, k].astype(F32)).astype(BF)
            planes[m].start(o, plane_out.at[m, o])
        plane_own[m] = wg[m, core, chip] + core_in[m, chip].astype(F32)

    def ring_send(m):
        value = plane_own[m]
        for o in range(1, H):
            value = value + plane_in[m, planes[m].take(o)].astype(F32)
        if split:
            value = value.reshape(N, rr, W)
            part[m] = value
            part_out[m] = value.astype(BF)
            for o in range(1, N):
                rings[m].start(o, part_out.at[m, rings[m].peer(o)])
        else:
            ring_in[m, me] = value.astype(BF)
            for o in range(1, N):
                rings[m].start(o, ring_in.at[m, me])

    def full_send(m):
        if split:
            value = part[m, me]
            for o in range(1, N):
                value = value + ring_in[m, rings[m].take(o)].astype(F32)
            full[m, me] = value.astype(BF)
            for o in range(1, N):
                fulls[m].start(o, full.at[m, me])

    def result(m, out):
        if split:
            for o in range(1, N):
                fulls[m].take(o)
            out[...] = full[m].astype(F32).reshape(r, W)
        else:
            for o in range(1, N):
                rings[m].take(o)
            out[...] = jnp.sum(ring_in[m].astype(F32), axis=0)

    weight_grad(0, img_t, img_back)
    fi[0:PI, :] = nt(img_back[0:PI, :], wi[...]).astype(BF)
    plane_send(0)

    grad = own_term[...]
    for o in range(1, N):
        grad = grad + term_in[term_x.take(o)].astype(F32)
    txt_back[...] = back_unit(grad, txt_unit[...], txt_inv[...]).astype(BF)
    weight_grad(1, txt_t, txt_back)
    ft[...] = nt(txt_back[...], wt[...]).astype(BF)
    save_txt = pltpu.make_async_copy(ft, ft_hbm, save_sem.at[1])
    save_txt.start()
    plane_send(1)
    for i in range(1, L):
        rows = slice(i * PI, (i + 1) * PI)
        fi[rows, :] = nt(img_back[rows, :], wi[...]).astype(BF)
    save_img = pltpu.make_async_copy(fi, fi_hbm, save_sem.at[0])
    save_img.start()
    ring_send(0)
    ring_send(1)
    full_send(0)
    full_send(1)
    result(0, gi_out)
    result(1, gt_out)

    save_img.wait()
    save_txt.wait()
    for copy in cores:
        copy.wait_send()
    for exchange in [text_x, term_x] + planes + rings + fulls:
        exchange.finish()


def shards(n_dp, n_neg, img_features, txt_features, w_img, w_txt, cap_len, pairs):
    L, PI, D = img_features.shape
    T = txt_features.shape[1]
    W = w_img.shape[1]
    N, H, r = n_neg, n_dp // 2, D // n_dp
    rows_i, rows_t = L * PI, L * T
    rr = r // N if r % (16 * N) == 0 else r
    vmem, dma = pltpu.VMEM, pltpu.SemaphoreType.DMA
    scratch = [
        vmem((rows_i, D), BF), vmem((rows_t, D), BF), vmem((D, W), BF), vmem((D, W), BF),
        vmem((D, rows_i), BF), vmem((D, rows_t), BF),
        vmem((rows_i, W), F32), vmem((rows_i, 1), F32), vmem((rows_i, W), BF),
        vmem((rows_t, W), F32), vmem((rows_t, 1), F32),
        vmem((N, rows_t, W), BF), vmem((N, rows_t, rows_i), F32), vmem((N, 8, rows_i), F32),
        vmem((N, N, 8, 128), F32), vmem((N, rows_t, rows_i), BF),
        vmem((N, rows_t, W), BF), vmem((rows_t, W), F32), vmem((N, rows_t, W), BF),
        vmem((rows_i, W), BF), vmem((rows_t, W), BF),
        vmem((2, 2, H, r, W), F32), vmem((2, H, r, W), BF), vmem((2, H, r, W), BF),
        vmem((2, H, r, W), BF), vmem((2, r, W), F32), vmem((2, H, r, W), BF),
        vmem((2, N, rr, W), F32), vmem((2, N, rr, W), BF),
        vmem((2, N, rr, W), BF), vmem((2, N, rr, W), BF),
        vmem((rows_i, D), BF), vmem((rows_t, D), BF),
        dma((4,)), dma((2,)),
        dma((N,)), dma((N,)), dma((N,)), dma((N,)), dma((N,)), dma((N,)),
        dma((2,)), dma((2,)), dma((2, H)), dma((2, H)),
        dma((2, N)), dma((2, N)), dma((2, N)), dma((2, N)),
    ]
    feat_img, feat_txt, final_img, final_txt = pl.pallas_call(
        functools.partial(kernel, (L, PI, T, D, W, N, n_dp)),
        out_shape=(
            jax.ShapeDtypeStruct((rows_i, D), BF),
            jax.ShapeDtypeStruct((rows_t, D), BF),
            jax.ShapeDtypeStruct((r, W), F32),
            jax.ShapeDtypeStruct((r, W), F32),
        ),
        in_specs=[pl.BlockSpec(memory_space=pl.ANY)] * 4
        + [pl.BlockSpec(memory_space=pltpu.SMEM)] * 2,
        out_specs=(pl.BlockSpec(memory_space=pl.ANY),) * 2
        + (pl.BlockSpec(memory_space=pltpu.VMEM),) * 2,
        scratch_shapes=scratch,
        compiler_params=pltpu.CompilerParams(
            collective_id=0, has_side_effects=True, vmem_limit_bytes=48 * 1024 * 1024
        ),
    )(
        img_features.reshape(rows_i, D),
        txt_features.reshape(rows_t, D),
        w_img,
        w_txt,
        cap_len,
        pairs,
    )
    return (
        feat_img.reshape(img_features.shape),
        feat_txt.reshape(txt_features.shape),
        final_img,
        final_txt,
    )


def solution(mesh):
    in_specs = (
        P(("dp", "neg"), None, None),
        P(("dp", "neg"), None, None),
        P(),
        P(),
        P(("dp", "neg")),
        P("dp", None),
    )
    out_specs = (
        P(("dp", "neg"), None, None),
        P(("dp", "neg"), None, None),
        P("dp", None),
        P("dp", None),
    )
    body = functools.partial(shards, mesh.shape["dp"], mesh.shape["neg"])
    return jax.shard_map(body, mesh=mesh, in_specs=in_specs, out_specs=out_specs, check_vma=False)
```

```python
import functools

import jax
import jax.numpy as jnp
from jax import lax
from jax.experimental import pallas as pl
from jax.experimental.pallas import tpu as pltpu
from jax.sharding import PartitionSpec as P

TOKEN_SCALE = 100.0
PAIR_SCALE = 50.0
EPSILON = 1e-06
MARK = 4.0
LOW = -1e30
VMEM_BYTES = 60 * 1024 * 1024
BF = jnp.bfloat16
F32 = jnp.float32
MESH = pl.DeviceIdType.MESH


def nn(a, b):
    return lax.dot_general(a, b, (((1,), (0,)), ((), ())), preferred_element_type=F32)


def nt(a, b):
    return lax.dot_general(a, b, (((1,), (1,)), ((), ())), preferred_element_type=F32)


def unit_rows(projected):
    inverse = lax.rsqrt(jnp.sum(projected * projected, axis=-1, keepdims=True) + EPSILON)
    return projected * inverse, inverse


def back_unit(gradient, unit, inverse):
    return (gradient - unit * jnp.sum(unit * gradient, axis=-1, keepdims=True)) * inverse


class Exchange:
    def __init__(self, me, n, device, slots, send, recv):
        self.me, self.n, self.device = me, n, device
        self.slots, self.send, self.recv = slots, send, recv
        self.started = []

    def peer(self, offset):
        return lax.rem(self.me + offset, self.n)

    def start(self, offset, source):
        copy = pltpu.make_async_remote_copy(
            src_ref=source,
            dst_ref=self.slots.at[self.me],
            send_sem=self.send.at[offset],
            recv_sem=self.recv.at[self.me],
            device_id=self.device(self.peer(offset)),
            device_id_type=MESH,
        )
        copy.start()
        self.started.append(copy)

    def take(self, offset):
        other = self.peer(offset)
        pltpu.make_async_remote_copy(
            src_ref=self.slots.at[other],
            dst_ref=self.slots.at[other],
            send_sem=self.send.at[offset],
            recv_sem=self.recv.at[other],
            device_id=self.device(other),
            device_id_type=MESH,
        ).wait_recv()
        return other

    def finish(self):
        for copy in self.started:
            copy.wait_send()


def kernel(
    dims,
    img_hbm, txt_hbm, wi_hbm, wt_hbm, cap, pairs,
    fi_hbm, ft_hbm, gi_hbm, gt_hbm,
    img, txt, wi, wt, img_t, txt_t,
    img_unit, img_inv, img_half, txt_unit, txt_inv,
    text_all, expo, total, logit_all, sg, terms, own_term, term_in,
    img_back, txt_back, wg, core_out, core_in, plane_out, plane_own, plane_in,
    part, part_out, ring_in, full, fi, ft, grads,
    load_sem, save_sem,
    text_s, text_r, logit_s, logit_r, term_s, term_r,
    core_s, core_r, plane_s, plane_r, ring_s, ring_r, full_s, full_r,
):
    L, PI, T, D, W, N, NDP = dims
    H = NDP // 2
    r = D // NDP
    rows_i, rows_t = L * PI, L * T
    dp = lax.axis_index("dp")
    me = lax.axis_index("neg")
    core = lax.rem(dp, 2)
    chip = lax.div(dp, 2)
    split = r % (16 * N) == 0
    rr = r // N if split else r

    loads = [
        pltpu.make_async_copy(source, target, load_sem.at[i])
        for i, (source, target) in enumerate(
            ((txt_hbm, txt), (wt_hbm, wt), (wi_hbm, wi), (img_hbm, img))
        )
    ]
    for load in loads:
        load.start()

    def on_neg(k):
        return (dp, k)

    def on_plane(k):
        return (k * 2 + core, me)

    barrier = pltpu.get_barrier_semaphore()
    for o in range(1, N):
        pl.semaphore_signal(barrier, inc=1, device_id=on_neg(lax.rem(me + o, N)), device_id_type=MESH)
    for o in range(1, H):
        pl.semaphore_signal(
            barrier, inc=1, device_id=on_plane(lax.rem(chip + o, H)), device_id_type=MESH
        )
    mate = (chip * 2 + 1 - core, me)
    pl.semaphore_signal(barrier, inc=1, device_id=mate, device_id_type=MESH)

    loads[0].wait()
    loads[1].wait()
    unit, inverse = unit_rows(nn(txt[...], wt[...]))
    txt_unit[...] = unit
    txt_inv[...] = inverse
    place = lax.broadcasted_iota(jnp.int32, (T, W), 0)
    for c in range(L):
        text_all[me, c * T:(c + 1) * T, :] = jnp.where(
            place < cap[c], unit[c * T:(c + 1) * T], MARK
        ).astype(BF)
    pl.semaphore_wait(barrier, N - 1 + H - 1 + 1)
    text_x = Exchange(me, N, on_neg, text_all, text_s, text_r)
    for o in range(1, N):
        text_x.start(o, text_all.at[me])

    loads[2].wait()
    loads[3].wait()
    for i in range(L):
        rows = slice(i * PI, (i + 1) * PI)
        unit, inverse = unit_rows(nn(img[rows, :], wi[...]))
        img_unit[rows, :] = unit
        img_inv[rows, :] = inverse
        img_half[rows, :] = unit.astype(BF)

    def transpose_features(features, features_t, start, size):
        step = max(256, r)
        for d in range(0, D, step):
            turned = features[start:start + size, d:d + step].T
            for k in range(d // r, (d + step) // r):
                at = k // 2 * r
                features_t[k % 2, at:at + r, start:start + size] = turned[k * r - d:(k + 1) * r - d]

    lane = lax.broadcasted_iota(jnp.int32, (8, 128), 1)
    line = lax.broadcasted_iota(jnp.int32, (8, 128), 0)

    def pool(j):
        text = text_all[j]
        marks = text[:, 0:128].astype(F32)
        marks = jnp.concatenate([marks] * (rows_i // 128), axis=1)
        scores = jnp.where(marks < 2.0, TOKEN_SCALE * nt(text, img_half[...]), LOW)
        scores = scores.reshape(L, T, rows_i)
        peaks = jnp.max(scores, axis=1, keepdims=True)
        expos = jnp.exp(scores - peaks)
        totals = jnp.sum(expos, axis=1)
        expo[j] = expos.reshape(rows_t, rows_i)
        total[j] = jnp.concatenate([totals, jnp.ones((8 - L, rows_i), F32)], axis=0)
        pooled = peaks[:, 0, :] + jnp.log(totals)
        pooled = jnp.concatenate([pooled, jnp.zeros((8 - L, rows_i), F32)], axis=0)
        tile = jnp.full((8, 128), LOW, F32)
        for i in range(L):
            mean = jnp.sum(pooled[:, i * PI:(i + 1) * PI], axis=1, keepdims=True)
            mean = mean * (PAIR_SCALE / (TOKEN_SCALE * PI))
            tile = jnp.where((lane == i) & (line < L), mean, tile)
        logit_all[me, j] = tile

    pool(me)
    transpose_features(img, img_t, 0, PI)
    for o in range(1, N):
        pool(text_x.take(o))
    logit_x = Exchange(me, N, on_neg, logit_all, logit_s, logit_r)
    for o in range(1, N):
        logit_x.start(o, logit_all.at[me])
    transpose_features(txt, txt_t, 0, rows_t)
    for i in range(1, L):
        transpose_features(img, img_t, i * PI, PI)
    own = logit_all[me]
    row_top = jnp.max(jnp.max(own, axis=0), axis=0, keepdims=True)
    row_exp = jnp.exp(own - row_top[None])
    row_prob = row_exp / jnp.sum(jnp.sum(row_exp, axis=0), axis=0, keepdims=True)[None]
    caption = lax.broadcasted_iota(jnp.int32, (N, 8, 128), 0) * L + lax.broadcasted_iota(
        jnp.int32, (N, 8, 128), 1
    )
    lanes = lax.broadcasted_iota(jnp.int32, (N, 8, 128), 2)
    target = jnp.zeros((N, 8, 128), F32)
    for i in range(L):
        target = jnp.where((lanes == i) & (caption == pairs[0, me * L + i]), 1.0, target)
    for o in range(1, N):
        logit_x.take(o)
    everyone = logit_all[...]
    col_top = jnp.max(jnp.max(everyone, axis=0), axis=-1, keepdims=True)
    col_sum = jnp.sum(
        jnp.sum(jnp.exp(everyone - col_top[None]), axis=0), axis=-1, keepdims=True
    )
    col_prob = jnp.exp(own - col_top) / col_sum
    pair_grad = (row_prob + col_prob - 2.0 * target) * (PAIR_SCALE / (2.0 * N * L * PI))
    own_logits = logit_all.at[me]
    logit_x.finish()
    own_logits[...] = pair_grad

    term_x = Exchange(me, N, on_neg, term_in, term_s, term_r)
    for o in list(range(1, N)) + [0]:
        j = lax.rem(me + o, N)
        pair = own_logits[j]
        spread = jnp.concatenate(
            [jnp.broadcast_to(pair[:, i:i + 1], (8, PI)) for i in range(L)], axis=1
        )
        factor = spread / total[j]
        shares = []
        for c in range(L):
            shares.append((expo[j, c * T:(c + 1) * T, :] * factor[c:c + 1, :]).astype(BF))
        share = jnp.concatenate(shares, axis=0)
        sg[j] = share
        term = nn(share, img_half[...])
        if o == 0:
            own_term[...] = term
        else:
            terms[o] = term.astype(BF)
            term_x.start(o, terms.at[o])

    texts = text_all[...].reshape(N * rows_t, W)
    for i in range(L):
        rows = slice(i * PI, (i + 1) * PI)
        grad = nn(sg[:, :, rows].reshape(N * rows_t, PI).T, texts)
        img_back[rows, :] = back_unit(grad, img_unit[rows, :], img_inv[rows, :]).astype(BF)

    cores = []

    def core_copy(m):
        return pltpu.make_async_remote_copy(
            src_ref=core_out.at[m],
            dst_ref=core_in.at[m],
            send_sem=core_s.at[m],
            recv_sem=core_r.at[m],
            device_id=mate,
            device_id_type=MESH,
        )

    def weight_grad(m, features_t, back):
        step = max(256, r)
        for d in range(0, H * r, step):
            out = nn(features_t[1 - core, d:d + step, :], back[...]).astype(BF)
            core_out[m, d // r:(d + step) // r] = out.reshape(step // r, r, W)
        copy = core_copy(m)
        copy.start()
        cores.append(copy)
        for d in range(0, H * r, step):
            out = nn(features_t[core, d:d + step, :], back[...])
            wg[m, d // r:(d + step) // r] = out.reshape(step // r, r, W)

    planes = [
        Exchange(chip, H, on_plane, plane_in.at[m], plane_s.at[m], plane_r.at[m]) for m in range(2)
    ]
    rings = [Exchange(me, N, on_neg, ring_in.at[m], ring_s.at[m], ring_r.at[m]) for m in range(2)]
    fulls = [Exchange(me, N, on_neg, full.at[m], full_s.at[m], full_r.at[m]) for m in range(2)]

    def plane_send(m):
        cores[m].wait_recv()
        for o in range(1, H):
            k = planes[m].peer(o)
            plane_out[m, o] = (wg[m, k] + core_in[m, k].astype(F32)).astype(BF)
            planes[m].start(o, plane_out.at[m, o])
        plane_own[m] = wg[m, chip] + core_in[m, chip].astype(F32)

    def ring_send(m):
        value = plane_own[m]
        for o in range(1, H):
            value = value + plane_in[m, planes[m].take(o)].astype(F32)
        if split:
            value = value.reshape(N, rr, W)
            part[m] = value
            part_out[m] = value.astype(BF)
            for o in range(1, N):
                rings[m].start(o, part_out.at[m, rings[m].peer(o)])
        else:
            ring_in[m, me] = value.astype(BF)
            for o in range(1, N):
                rings[m].start(o, ring_in.at[m, me])

    def full_send(m):
        if split:
            value = part[m, me]
            for o in range(1, N):
                value = value + ring_in[m, rings[m].take(o)].astype(F32)
            full[m, me] = value.astype(BF)
            for o in range(1, N):
                fulls[m].start(o, full.at[m, me])

    saves = []

    def save(i, source, target):
        copy = pltpu.make_async_copy(source, target, save_sem.at[i])
        copy.start()
        saves.append(copy)

    def result(m, out):
        if split:
            for o in range(1, N):
                fulls[m].take(o)
            grads[m] = full[m].astype(F32).reshape(r, W)
        else:
            for o in range(1, N):
                rings[m].take(o)
            grads[m] = jnp.sum(ring_in[m].astype(F32), axis=0)
        save(2 + m, grads.at[m], out)

    weight_grad(0, img_t, img_back)
    fi[0:PI, :] = nt(img_back[0:PI, :], wi[...]).astype(BF)
    plane_send(0)

    grad = own_term[...]
    for o in range(1, N):
        grad = grad + term_in[term_x.take(o)].astype(F32)
    txt_back[...] = back_unit(grad, txt_unit[...], txt_inv[...]).astype(BF)
    weight_grad(1, txt_t, txt_back)
    ring_send(0)
    plane_send(1)
    ft[...] = nt(txt_back[...], wt[...]).astype(BF)
    save(1, ft, ft_hbm)
    full_send(0)
    for i in range(1, L):
        rows = slice(i * PI, (i + 1) * PI)
        fi[rows, :] = nt(img_back[rows, :], wi[...]).astype(BF)
    save(0, fi, fi_hbm)
    ring_send(1)
    result(0, gi_hbm)
    full_send(1)
    result(1, gt_hbm)

    for copy in cores:
        copy.wait_send()
    for copy in saves:
        copy.wait()
    for exchange in [text_x, term_x] + planes + rings + fulls:
        exchange.finish()


def write_out(*refs):
    sources, targets, sems = refs[:4], refs[4:8], refs[8]
    copies = []
    for source, target in zip(sources, targets):
        rows = source.shape[0]
        step = rows // 4 if rows % 64 == 0 and source.dtype == BF else rows
        for at in range(0, rows, step):
            piece = pl.ds(at, step)
            copies.append(
                pltpu.make_async_copy(source.at[piece], target.at[piece], sems.at[len(copies)])
            )
    for copy in copies:
        copy.start()
    for copy in copies:
        copy.wait()


def shards(n_dp, n_neg, img_features, txt_features, w_img, w_txt, cap_len, pairs):
    L, PI, D = img_features.shape
    T = txt_features.shape[1]
    W = w_img.shape[1]
    N, H, r = n_neg, n_dp // 2, D // n_dp
    rows_i, rows_t = L * PI, L * T
    rr = r // N if r % (16 * N) == 0 else r
    vmem, dma = pltpu.VMEM, pltpu.SemaphoreType.DMA
    scratch = [
        vmem((rows_i, D), BF), vmem((rows_t, D), BF), vmem((D, W), BF), vmem((D, W), BF),
        vmem((2, H * r, rows_i), BF), vmem((2, H * r, rows_t), BF),
        vmem((rows_i, W), F32), vmem((rows_i, 1), F32), vmem((rows_i, W), BF),
        vmem((rows_t, W), F32), vmem((rows_t, 1), F32),
        vmem((N, rows_t, W), BF), vmem((N, rows_t, rows_i), F32), vmem((N, 8, rows_i), F32),
        vmem((N, N, 8, 128), F32), vmem((N, rows_t, rows_i), BF),
        vmem((N, rows_t, W), BF), vmem((rows_t, W), F32), vmem((N, rows_t, W), BF),
        vmem((rows_i, W), BF), vmem((rows_t, W), BF),
        vmem((2, H, r, W), F32), vmem((2, H, r, W), BF), vmem((2, H, r, W), BF),
        vmem((2, H, r, W), BF), vmem((2, r, W), F32), vmem((2, H, r, W), BF),
        vmem((2, N, rr, W), F32), vmem((2, N, rr, W), BF),
        vmem((2, N, rr, W), BF), vmem((2, N, rr, W), BF),
        vmem((rows_i, D), BF), vmem((rows_t, D), BF), vmem((2, r, W), F32),
        dma((4,)), dma((4,)),
        dma((N,)), dma((N,)), dma((N,)), dma((N,)), dma((N,)), dma((N,)),
        dma((2,)), dma((2,)), dma((2, H)), dma((2, H)),
        dma((2, N)), dma((2, N)), dma((2, N)), dma((2, N)),
    ]
    shapes = (
        jax.ShapeDtypeStruct((rows_i, D), BF),
        jax.ShapeDtypeStruct((rows_t, D), BF),
        jax.ShapeDtypeStruct((r, W), F32),
        jax.ShapeDtypeStruct((r, W), F32),
    )
    results = pl.pallas_call(
        functools.partial(kernel, (L, PI, T, D, W, N, n_dp)),
        out_shape=shapes,
        in_specs=[pl.BlockSpec(memory_space=pltpu.HBM)] * 4
        + [pl.BlockSpec(memory_space=pltpu.SMEM)] * 2,
        out_specs=(pl.BlockSpec(memory_space=pltpu.HBM),) * 4,
        scratch_shapes=scratch,
        compiler_params=pltpu.CompilerParams(
            collective_id=0, has_side_effects=True, vmem_limit_bytes=VMEM_BYTES
        ),
    )(
        img_features.reshape(rows_i, D),
        txt_features.reshape(rows_t, D),
        w_img,
        w_txt,
        cap_len,
        pairs,
    )
    feat_img, feat_txt, final_img, final_txt = pl.pallas_call(
        write_out,
        out_shape=shapes,
        in_specs=[pl.BlockSpec(memory_space=pl.ANY)] * 4,
        out_specs=(pl.BlockSpec(memory_space=pltpu.HBM),) * 4,
        scratch_shapes=[dma((16,))],
        compiler_params=pltpu.CompilerParams(vmem_limit_bytes=VMEM_BYTES),
    )(*results)
    return (
        feat_img.reshape(img_features.shape),
        feat_txt.reshape(txt_features.shape),
        final_img,
        final_txt,
    )


def solution(mesh):
    in_specs = (
        P(("dp", "neg"), None, None),
        P(("dp", "neg"), None, None),
        P(),
        P(),
        P(("dp", "neg")),
        P("dp", None),
    )
    out_specs = (
        P(("dp", "neg"), None, None),
        P(("dp", "neg"), None, None),
        P("dp", None),
        P("dp", None),
    )
    body = functools.partial(shards, mesh.shape["dp"], mesh.shape["neg"])
    return jax.shard_map(body, mesh=mesh, in_specs=in_specs, out_specs=out_specs, check_vma=False)
```

```python
import functools

import jax
import jax.numpy as jnp
from jax import lax
from jax.experimental import pallas as pl
from jax.experimental.pallas import tpu as pltpu
from jax.sharding import PartitionSpec as P

TOKEN_SCALE = 100.0
PAIR_SCALE = 50.0
EPSILON = 1e-06
MARK = 4.0
LOW = -1e30
VMEM_BYTES = 60 * 1024 * 1024
BF = jnp.bfloat16
F32 = jnp.float32
MESH = pl.DeviceIdType.MESH


def nn(a, b):
    return lax.dot_general(a, b, (((1,), (0,)), ((), ())), preferred_element_type=F32)


def nt(a, b):
    return lax.dot_general(a, b, (((1,), (1,)), ((), ())), preferred_element_type=F32)


def unit_rows(projected):
    inverse = lax.rsqrt(jnp.sum(projected * projected, axis=-1, keepdims=True) + EPSILON)
    return projected * inverse, inverse


def back_unit(gradient, unit, inverse):
    return (gradient - unit * jnp.sum(unit * gradient, axis=-1, keepdims=True)) * inverse


class Exchange:
    def __init__(self, me, n, device, slots, send, recv, line=True):
        self.me, self.n, self.device, self.line = me, n, device, line
        self.slots, self.send, self.recv = slots, send, recv
        self.started = []

    def peer(self, offset):
        if not self.line:
            return lax.rem(self.me + offset, self.n)
        upper = lax.div(self.me * 2, self.n)
        k = upper * (offset - 1) + (1 - upper) * (self.n - 1 - offset)
        return k + lax.div(k + self.n - self.me, self.n)

    def start(self, offset, source):
        copy = pltpu.make_async_remote_copy(
            src_ref=source,
            dst_ref=self.slots.at[self.me],
            send_sem=self.send.at[offset],
            recv_sem=self.recv.at[self.me],
            device_id=self.device(self.peer(offset)),
            device_id_type=MESH,
        )
        copy.start()
        self.started.append(copy)

    def take(self, offset):
        other = self.peer(offset)
        pltpu.make_async_remote_copy(
            src_ref=self.slots.at[other],
            dst_ref=self.slots.at[other],
            send_sem=self.send.at[offset],
            recv_sem=self.recv.at[other],
            device_id=self.device(other),
            device_id_type=MESH,
        ).wait_recv()
        return other

    def finish(self):
        for copy in self.started:
            copy.wait_send()


def kernel(
    dims,
    img_hbm, txt_hbm, wi_hbm, wt_hbm, cap, pairs,
    fi_hbm, ft_hbm, gi_hbm, gt_hbm,
    img, txt, wi, wt, img_t, txt_t,
    img_unit, img_inv, img_half, txt_unit, txt_inv,
    text_all, expo, total, logit_all, sg, terms, own_term, term_in,
    img_back, txt_back, wg, core_out, core_in, plane_out, plane_own, plane_in,
    part, part_out, ring_in, full, fi, ft, grads,
    load_sem, save_sem,
    text_s, text_r, logit_s, logit_r, term_s, term_r,
    core_s, core_r, plane_s, plane_r, ring_s, ring_r, full_s, full_r,
):
    L, PI, T, D, W, N, NDP = dims
    H = NDP // 2
    r = D // NDP
    rows_i, rows_t = L * PI, L * T
    dp = lax.axis_index("dp")
    me = lax.axis_index("neg")
    core = lax.rem(dp, 2)
    chip = lax.div(dp, 2)
    split = r % (16 * N) == 0
    rr = r // N if split else r

    loads = [
        pltpu.make_async_copy(source, target, load_sem.at[i])
        for i, (source, target) in enumerate(
            ((txt_hbm, txt), (wt_hbm, wt), (wi_hbm, wi), (img_hbm, img))
        )
    ]
    for load in loads:
        load.start()

    def on_neg(k):
        return (dp, k)

    def on_plane(k):
        return (k * 2 + core, me)

    barrier = pltpu.get_barrier_semaphore()
    for o in range(1, N):
        pl.semaphore_signal(barrier, inc=1, device_id=on_neg(lax.rem(me + o, N)), device_id_type=MESH)
    for o in range(1, H):
        pl.semaphore_signal(
            barrier, inc=1, device_id=on_plane(lax.rem(chip + o, H)), device_id_type=MESH
        )
    mate = (chip * 2 + 1 - core, me)
    pl.semaphore_signal(barrier, inc=1, device_id=mate, device_id_type=MESH)

    loads[0].wait()
    loads[1].wait()
    unit, inverse = unit_rows(nn(txt[...], wt[...]))
    txt_unit[...] = unit
    txt_inv[...] = inverse
    place = lax.broadcasted_iota(jnp.int32, (T, W), 0)
    for c in range(L):
        text_all[me, c * T:(c + 1) * T, :] = jnp.where(
            place < cap[c], unit[c * T:(c + 1) * T], MARK
        ).astype(BF)
    pl.semaphore_wait(barrier, N - 1 + H - 1 + 1)
    text_x = Exchange(me, N, on_neg, text_all, text_s, text_r)
    for o in range(1, N):
        text_x.start(o, text_all.at[me])

    loads[2].wait()
    loads[3].wait()
    for i in range(L):
        rows = slice(i * PI, (i + 1) * PI)
        unit, inverse = unit_rows(nn(img[rows, :], wi[...]))
        img_unit[rows, :] = unit
        img_inv[rows, :] = inverse
        img_half[rows, :] = unit.astype(BF)

    def transpose_features(features, features_t, start, size):
        step = max(256, r)
        for d in range(0, D, step):
            turned = features[start:start + size, d:d + step].T
            for k in range(d // r, (d + step) // r):
                at = k // 2 * r
                features_t[k % 2, at:at + r, start:start + size] = turned[k * r - d:(k + 1) * r - d]

    lane = lax.broadcasted_iota(jnp.int32, (8, 128), 1)
    line = lax.broadcasted_iota(jnp.int32, (8, 128), 0)

    def pool(j):
        text = text_all[j]
        marks = text[:, 0:128].astype(F32)
        marks = jnp.concatenate([marks] * (rows_i // 128), axis=1)
        scores = jnp.where(marks < 2.0, TOKEN_SCALE * nt(text, img_half[...]), LOW)
        scores = scores.reshape(L, T, rows_i)
        peaks = jnp.max(scores, axis=1, keepdims=True)
        expos = jnp.exp(scores - peaks)
        totals = jnp.sum(expos, axis=1)
        expo[j] = expos.reshape(rows_t, rows_i)
        total[j] = jnp.concatenate([totals, jnp.ones((8 - L, rows_i), F32)], axis=0)
        pooled = peaks[:, 0, :] + jnp.log(totals)
        pooled = jnp.concatenate([pooled, jnp.zeros((8 - L, rows_i), F32)], axis=0)
        tile = jnp.full((8, 128), LOW, F32)
        for i in range(L):
            mean = jnp.sum(pooled[:, i * PI:(i + 1) * PI], axis=1, keepdims=True)
            mean = mean * (PAIR_SCALE / (TOKEN_SCALE * PI))
            tile = jnp.where((lane == i) & (line < L), mean, tile)
        logit_all[me, j] = tile

    pool(me)
    transpose_features(img, img_t, 0, PI)
    for o in reversed(range(1, N)):
        pool(text_x.take(o))
    logit_x = Exchange(me, N, on_neg, logit_all, logit_s, logit_r)
    for o in range(1, N):
        logit_x.start(o, logit_all.at[me])
    transpose_features(txt, txt_t, 0, rows_t)
    for i in range(1, L):
        transpose_features(img, img_t, i * PI, PI)
    own = logit_all[me]
    row_top = jnp.max(jnp.max(own, axis=0), axis=0, keepdims=True)
    row_exp = jnp.exp(own - row_top[None])
    row_prob = row_exp / jnp.sum(jnp.sum(row_exp, axis=0), axis=0, keepdims=True)[None]
    caption = lax.broadcasted_iota(jnp.int32, (N, 8, 128), 0) * L + lax.broadcasted_iota(
        jnp.int32, (N, 8, 128), 1
    )
    lanes = lax.broadcasted_iota(jnp.int32, (N, 8, 128), 2)
    target = jnp.zeros((N, 8, 128), F32)
    for i in range(L):
        target = jnp.where((lanes == i) & (caption == pairs[0, me * L + i]), 1.0, target)
    for o in range(1, N):
        logit_x.take(o)
    everyone = logit_all[...]
    col_top = jnp.max(jnp.max(everyone, axis=0), axis=-1, keepdims=True)
    col_sum = jnp.sum(
        jnp.sum(jnp.exp(everyone - col_top[None]), axis=0), axis=-1, keepdims=True
    )
    col_prob = jnp.exp(own - col_top) / col_sum
    pair_grad = (row_prob + col_prob - 2.0 * target) * (PAIR_SCALE / (2.0 * N * L * PI))
    own_logits = logit_all.at[me]
    logit_x.finish()
    own_logits[...] = pair_grad

    term_x = Exchange(me, N, on_neg, term_in, term_s, term_r)
    for o in list(range(1, N)) + [0]:
        j = term_x.peer(o) if o else me
        pair = own_logits[j]
        spread = jnp.concatenate(
            [jnp.broadcast_to(pair[:, i:i + 1], (8, PI)) for i in range(L)], axis=1
        )
        factor = spread / total[j]
        shares = []
        for c in range(L):
            shares.append((expo[j, c * T:(c + 1) * T, :] * factor[c:c + 1, :]).astype(BF))
        share = jnp.concatenate(shares, axis=0)
        sg[j] = share
        term = nn(share, img_half[...])
        if o == 0:
            own_term[...] = term
        else:
            terms[o] = term.astype(BF)
            term_x.start(o, terms.at[o])

    texts = text_all[...].reshape(N * rows_t, W)
    for i in range(L):
        rows = slice(i * PI, (i + 1) * PI)
        grad = nn(sg[:, :, rows].reshape(N * rows_t, PI).T, texts)
        img_back[rows, :] = back_unit(grad, img_unit[rows, :], img_inv[rows, :]).astype(BF)

    cores = []

    def core_copy(m):
        return pltpu.make_async_remote_copy(
            src_ref=core_out.at[m],
            dst_ref=core_in.at[m],
            send_sem=core_s.at[m],
            recv_sem=core_r.at[m],
            device_id=mate,
            device_id_type=MESH,
        )

    def weight_grad(m, features_t, back):
        step = max(256, r)
        for d in range(0, H * r, step):
            out = nn(features_t[1 - core, d:d + step, :], back[...]).astype(BF)
            core_out[m, d // r:(d + step) // r] = out.reshape(step // r, r, W)
        copy = core_copy(m)
        copy.start()
        cores.append(copy)
        for d in range(0, H * r, step):
            out = nn(features_t[core, d:d + step, :], back[...])
            wg[m, d // r:(d + step) // r] = out.reshape(step // r, r, W)

    planes = [
        Exchange(chip, H, on_plane, plane_in.at[m], plane_s.at[m], plane_r.at[m], line=False) for m in range(2)
    ]
    rings = [Exchange(me, N, on_neg, ring_in.at[m], ring_s.at[m], ring_r.at[m]) for m in range(2)]
    fulls = [Exchange(me, N, on_neg, full.at[m], full_s.at[m], full_r.at[m]) for m in range(2)]

    def plane_send(m):
        cores[m].wait_recv()
        for o in range(1, H):
            k = planes[m].peer(o)
            plane_out[m, o] = (wg[m, k] + core_in[m, k].astype(F32)).astype(BF)
            planes[m].start(o, plane_out.at[m, o])
        plane_own[m] = wg[m, chip] + core_in[m, chip].astype(F32)

    def ring_send(m):
        value = plane_own[m]
        for o in range(1, H):
            value = value + plane_in[m, planes[m].take(o)].astype(F32)
        if split:
            value = value.reshape(N, rr, W)
            part[m] = value
            part_out[m] = value.astype(BF)
            for o in range(1, N):
                rings[m].start(o, part_out.at[m, rings[m].peer(o)])
        else:
            ring_in[m, me] = value.astype(BF)
            for o in range(1, N):
                rings[m].start(o, ring_in.at[m, me])

    def full_send(m):
        if split:
            value = part[m, me]
            for o in range(1, N):
                value = value + ring_in[m, rings[m].take(o)].astype(F32)
            full[m, me] = value.astype(BF)
            for o in range(1, N):
                fulls[m].start(o, full.at[m, me])

    saves = []

    def save(i, source, target):
        copy = pltpu.make_async_copy(source, target, save_sem.at[i])
        copy.start()
        saves.append(copy)

    def result(m, out):
        if split:
            for o in range(1, N):
                fulls[m].take(o)
            grads[m] = full[m].astype(F32).reshape(r, W)
        else:
            for o in range(1, N):
                rings[m].take(o)
            grads[m] = jnp.sum(ring_in[m].astype(F32), axis=0)
        save(2 + m, grads.at[m], out)

    weight_grad(0, img_t, img_back)
    fi[0:PI, :] = nt(img_back[0:PI, :], wi[...]).astype(BF)
    plane_send(0)

    grad = own_term[...]
    for o in range(1, N):
        grad = grad + term_in[term_x.take(o)].astype(F32)
    txt_back[...] = back_unit(grad, txt_unit[...], txt_inv[...]).astype(BF)
    weight_grad(1, txt_t, txt_back)
    ring_send(0)
    plane_send(1)
    ft[...] = nt(txt_back[...], wt[...]).astype(BF)
    save(1, ft, ft_hbm)
    full_send(0)
    for i in range(1, L):
        rows = slice(i * PI, (i + 1) * PI)
        fi[rows, :] = nt(img_back[rows, :], wi[...]).astype(BF)
    save(0, fi, fi_hbm)
    ring_send(1)
    result(0, gi_hbm)
    full_send(1)
    result(1, gt_hbm)

    for copy in cores:
        copy.wait_send()
    for copy in saves:
        copy.wait()
    for exchange in [text_x, term_x] + planes + rings + fulls:
        exchange.finish()


def write_out(*refs):
    sources, targets, held, in_sem, out_sem = refs[:4], refs[4:8], refs[8:12], refs[12], refs[13]
    loads, saves = [], []
    for source, target, hold in zip(sources, targets, held):
        rows = source.shape[0]
        step = rows // 4 if rows % 64 == 0 and source.dtype == BF else rows
        for at in range(0, rows, step):
            piece, i = pl.ds(at, step), len(loads)
            loads.append(pltpu.make_async_copy(source.at[piece], hold.at[piece], in_sem.at[i]))
            saves.append(pltpu.make_async_copy(hold.at[piece], target.at[piece], out_sem.at[i]))
    for load in loads:
        load.start()
    for load, save in zip(loads, saves):
        load.wait()
        save.start()
    for save in saves:
        save.wait()


def shards(n_dp, n_neg, img_features, txt_features, w_img, w_txt, cap_len, pairs):
    L, PI, D = img_features.shape
    T = txt_features.shape[1]
    W = w_img.shape[1]
    N, H, r = n_neg, n_dp // 2, D // n_dp
    rows_i, rows_t = L * PI, L * T
    rr = r // N if r % (16 * N) == 0 else r
    vmem, dma = pltpu.VMEM, pltpu.SemaphoreType.DMA
    scratch = [
        vmem((rows_i, D), BF), vmem((rows_t, D), BF), vmem((D, W), BF), vmem((D, W), BF),
        vmem((2, H * r, rows_i), BF), vmem((2, H * r, rows_t), BF),
        vmem((rows_i, W), F32), vmem((rows_i, 1), F32), vmem((rows_i, W), BF),
        vmem((rows_t, W), F32), vmem((rows_t, 1), F32),
        vmem((N, rows_t, W), BF), vmem((N, rows_t, rows_i), F32), vmem((N, 8, rows_i), F32),
        vmem((N, N, 8, 128), F32), vmem((N, rows_t, rows_i), BF),
        vmem((N, rows_t, W), BF), vmem((rows_t, W), F32), vmem((N, rows_t, W), BF),
        vmem((rows_i, W), BF), vmem((rows_t, W), BF),
        vmem((2, H, r, W), F32), vmem((2, H, r, W), BF), vmem((2, H, r, W), BF),
        vmem((2, H, r, W), BF), vmem((2, r, W), F32), vmem((2, H, r, W), BF),
        vmem((2, N, rr, W), F32), vmem((2, N, rr, W), BF),
        vmem((2, N, rr, W), BF), vmem((2, N, rr, W), BF),
        vmem((rows_i, D), BF), vmem((rows_t, D), BF), vmem((2, r, W), F32),
        dma((4,)), dma((4,)),
        dma((N,)), dma((N,)), dma((N,)), dma((N,)), dma((N,)), dma((N,)),
        dma((2,)), dma((2,)), dma((2, H)), dma((2, H)),
        dma((2, N)), dma((2, N)), dma((2, N)), dma((2, N)),
    ]
    shapes = (
        jax.ShapeDtypeStruct((rows_i, D), BF),
        jax.ShapeDtypeStruct((rows_t, D), BF),
        jax.ShapeDtypeStruct((r, W), F32),
        jax.ShapeDtypeStruct((r, W), F32),
    )
    results = pl.pallas_call(
        functools.partial(kernel, (L, PI, T, D, W, N, n_dp)),
        out_shape=shapes,
        in_specs=[pl.BlockSpec(memory_space=pltpu.HBM)] * 4
        + [pl.BlockSpec(memory_space=pltpu.SMEM)] * 2,
        out_specs=(pl.BlockSpec(memory_space=pltpu.HBM),) * 4,
        scratch_shapes=scratch,
        compiler_params=pltpu.CompilerParams(
            collective_id=0, has_side_effects=True, vmem_limit_bytes=VMEM_BYTES
        ),
    )(
        img_features.reshape(rows_i, D),
        txt_features.reshape(rows_t, D),
        w_img,
        w_txt,
        cap_len,
        pairs,
    )
    feat_img, feat_txt, final_img, final_txt = pl.pallas_call(
        write_out,
        out_shape=shapes,
        in_specs=[pl.BlockSpec(memory_space=pl.ANY)] * 4,
        out_specs=(pl.BlockSpec(memory_space=pltpu.HBM),) * 4,
        scratch_shapes=[vmem(shape.shape, shape.dtype) for shape in shapes]
        + [dma((16,)), dma((16,))],
        compiler_params=pltpu.CompilerParams(vmem_limit_bytes=VMEM_BYTES),
    )(*results)
    return (
        feat_img.reshape(img_features.shape),
        feat_txt.reshape(txt_features.shape),
        final_img,
        final_txt,
    )


def solution(mesh):
    in_specs = (
        P(("dp", "neg"), None, None),
        P(("dp", "neg"), None, None),
        P(),
        P(),
        P(("dp", "neg")),
        P("dp", None),
    )
    out_specs = (
        P(("dp", "neg"), None, None),
        P(("dp", "neg"), None, None),
        P("dp", None),
        P("dp", None),
    )
    body = functools.partial(shards, mesh.shape["dp"], mesh.shape["neg"])
    return jax.shard_map(body, mesh=mesh, in_specs=in_specs, out_specs=out_specs, check_vma=False)
```

```python
import functools

import jax
import jax.numpy as jnp
from jax import lax
from jax.experimental import pallas as pl
from jax.experimental.pallas import tpu as pltpu
from jax.sharding import PartitionSpec as P

TOKEN_SCALE = 100.0
PAIR_SCALE = 50.0
EPSILON = 1e-06
MARK = 4.0
LOW = -1e30
VMEM_BYTES = 60 * 1024 * 1024
BF = jnp.bfloat16
F32 = jnp.float32
MESH = pl.DeviceIdType.MESH


def nn(a, b):
    return lax.dot_general(a, b, (((1,), (0,)), ((), ())), preferred_element_type=F32)


def nt(a, b):
    return lax.dot_general(a, b, (((1,), (1,)), ((), ())), preferred_element_type=F32)


def unit_rows(projected):
    inverse = lax.rsqrt(jnp.sum(projected * projected, axis=-1, keepdims=True) + EPSILON)
    return projected * inverse, inverse


def back_unit(gradient, unit, inverse):
    return (gradient - unit * jnp.sum(unit * gradient, axis=-1, keepdims=True)) * inverse


class Exchange:
    def __init__(self, me, n, device, slots, send, recv, line=True):
        self.me, self.n, self.device, self.line = me, n, device, line
        self.slots, self.send, self.recv = slots, send, recv
        self.started = []

    def peer(self, offset):
        if not self.line:
            return lax.rem(self.me + offset, self.n)
        upper = lax.div(self.me * 2, self.n)
        k = upper * (offset - 1) + (1 - upper) * (self.n - 1 - offset)
        return k + lax.div(k + self.n - self.me, self.n)

    def start(self, offset, source):
        copy = pltpu.make_async_remote_copy(
            src_ref=source,
            dst_ref=self.slots.at[self.me],
            send_sem=self.send.at[offset],
            recv_sem=self.recv.at[self.me],
            device_id=self.device(self.peer(offset)),
            device_id_type=MESH,
        )
        copy.start()
        self.started.append(copy)

    def take(self, offset):
        other = self.peer(offset)
        pltpu.make_async_remote_copy(
            src_ref=self.slots.at[other],
            dst_ref=self.slots.at[other],
            send_sem=self.send.at[offset],
            recv_sem=self.recv.at[other],
            device_id=self.device(other),
            device_id_type=MESH,
        ).wait_recv()
        return other

    def finish(self):
        for copy in self.started:
            copy.wait_send()


def kernel(
    dims,
    img_hbm, txt_hbm, wi_hbm, wt_hbm, cap, pairs,
    fi_hbm, ft_hbm, gi_hbm, gt_hbm,
    img, txt, wi, wt, img_t, txt_t,
    img_unit, img_inv, img_half, txt_unit, txt_inv,
    text_all, expo, total, logit_all, sg, terms, own_term, term_in,
    img_back, txt_back, wg, core_out, core_in, plane_out, plane_own, plane_in,
    part, part_out, ring_in, full, fi, ft, grads,
    load_sem, save_sem,
    text_s, text_r, logit_s, logit_r, term_s, term_r,
    core_s, core_r, plane_s, plane_r, ring_s, ring_r, full_s, full_r,
):
    L, PI, T, D, W, N, NDP = dims
    H = NDP // 2
    r = D // NDP
    rows_i, rows_t = L * PI, L * T
    dp = lax.axis_index("dp")
    me = lax.axis_index("neg")
    core = lax.rem(dp, 2)
    chip = lax.div(dp, 2)
    split = r % (16 * N) == 0
    rr = r // N if split else r

    loads = [
        pltpu.make_async_copy(source, target, load_sem.at[i])
        for i, (source, target) in enumerate(
            ((txt_hbm, txt), (wt_hbm, wt), (wi_hbm, wi), (img_hbm, img))
        )
    ]
    for load in loads:
        load.start()

    def on_neg(k):
        return (dp, k)

    def on_plane(k):
        return (k * 2 + core, me)

    barrier = pltpu.get_barrier_semaphore()
    for o in range(1, N):
        pl.semaphore_signal(barrier, inc=1, device_id=on_neg(lax.rem(me + o, N)), device_id_type=MESH)
    for o in range(1, H):
        pl.semaphore_signal(
            barrier, inc=1, device_id=on_plane(lax.rem(chip + o, H)), device_id_type=MESH
        )
    mate = (chip * 2 + 1 - core, me)
    pl.semaphore_signal(barrier, inc=1, device_id=mate, device_id_type=MESH)

    loads[0].wait()
    loads[1].wait()
    unit, inverse = unit_rows(nn(txt[...], wt[...]))
    txt_unit[...] = unit
    txt_inv[...] = inverse
    place = lax.broadcasted_iota(jnp.int32, (T, W), 0)
    for c in range(L):
        text_all[me, c * T:(c + 1) * T, :] = jnp.where(
            place < cap[c], unit[c * T:(c + 1) * T], MARK
        ).astype(BF)
    pl.semaphore_wait(barrier, N - 1 + H - 1 + 1)
    text_x = Exchange(me, N, on_neg, text_all, text_s, text_r)
    for o in range(1, N):
        text_x.start(o, text_all.at[me])

    loads[2].wait()
    loads[3].wait()
    for i in range(L):
        rows = slice(i * PI, (i + 1) * PI)
        unit, inverse = unit_rows(nn(img[rows, :], wi[...]))
        img_unit[rows, :] = unit
        img_inv[rows, :] = inverse
        img_half[rows, :] = unit.astype(BF)

    def transpose_features(features, features_t, start, size):
        step = max(256, r)
        for d in range(0, D, step):
            turned = features[start:start + size, d:d + step].T
            for k in range(d // r, (d + step) // r):
                at = k // 2 * r
                features_t[k % 2, at:at + r, start:start + size] = turned[k * r - d:(k + 1) * r - d]

    lane = lax.broadcasted_iota(jnp.int32, (8, 128), 1)
    line = lax.broadcasted_iota(jnp.int32, (8, 128), 0)

    def pool(j, tile):
        text = text_all[j]
        marks = text[:, 0:128].astype(F32)
        marks = jnp.concatenate([marks] * (rows_i // 128), axis=1)
        scores = jnp.where(marks < 2.0, TOKEN_SCALE * nt(text, img_half[...]), LOW)
        scores = scores.reshape(L, T, rows_i)
        peaks = jnp.max(scores, axis=1, keepdims=True)
        expos = jnp.exp(scores - peaks)
        totals = jnp.sum(expos, axis=1)
        expo[j] = expos.reshape(rows_t, rows_i)
        total[j] = jnp.concatenate([totals, jnp.ones((8 - L, rows_i), F32)], axis=0)
        pooled = peaks[:, 0, :] + jnp.log(totals)
        pooled = jnp.concatenate([pooled, jnp.zeros((8 - L, rows_i), F32)], axis=0)
        for i in range(L):
            mean = jnp.sum(pooled[:, i * PI:(i + 1) * PI], axis=1, keepdims=True)
            mean = mean * (PAIR_SCALE / (TOKEN_SCALE * PI))
            tile = jnp.where((lane == j * L + i) & (line < L), mean, tile)
        return tile

    tile = pool(me, jnp.full((8, 128), LOW, F32))
    for i in range(L):
        transpose_features(img, img_t, i * PI, PI)
    for o in reversed(range(1, N)):
        tile = pool(text_x.take(o), tile)
    logit_all[me] = tile
    logit_x = Exchange(me, N, on_neg, logit_all, logit_s, logit_r)
    for o in range(1, N):
        logit_x.start(o, logit_all.at[me])
    transpose_features(txt, txt_t, 0, rows_t)
    owner, image = lax.div(lane, L), lax.rem(lane, L)

    def over_images(value, reduce, fill):
        out = value
        for j in range(N):
            mine = owner == j
            total = reduce(jnp.where(mine, value, fill), axis=1, keepdims=True)
            out = jnp.where(mine, total, out)
        return out

    row_prob = jnp.zeros((8, 128), F32)
    target = jnp.zeros((8, 128), F32)
    for i in range(L):
        mine = image == i
        values = jnp.where(mine, tile, LOW)
        row_top = jnp.max(jnp.max(values, axis=1, keepdims=True), axis=0, keepdims=True)
        row_exp = jnp.exp(values - row_top)
        row_sum = jnp.sum(jnp.sum(row_exp, axis=1, keepdims=True), axis=0, keepdims=True)
        row_prob = jnp.where(mine, row_exp / row_sum, row_prob)
        hit = mine & (owner * L + line == pairs[0, me * L + i])
        target = jnp.where(hit, 1.0, target)
    for o in range(1, N):
        logit_x.take(o)
    everyone = logit_all[...]
    col_top = over_images(jnp.max(everyone, axis=0), jnp.max, LOW)
    col_sum = over_images(jnp.sum(jnp.exp(everyone - col_top[None]), axis=0), jnp.sum, 0.0)
    col_prob = jnp.exp(tile - col_top) / col_sum
    pair_grad = (row_prob + col_prob - 2.0 * target) * (PAIR_SCALE / (2.0 * N * L * PI))
    logit_x.finish()

    term_x = Exchange(me, N, on_neg, term_in, term_s, term_r)
    for o in list(range(1, N)) + [0]:
        j = term_x.peer(o) if o else me
        spread = jnp.concatenate(
            [
                jnp.broadcast_to(
                    jnp.sum(jnp.where(lane == j * L + i, pair_grad, 0.0), axis=1, keepdims=True),
                    (8, PI),
                )
                for i in range(L)
            ],
            axis=1,
        )
        factor = spread / total[j]
        shares = []
        for c in range(L):
            shares.append((expo[j, c * T:(c + 1) * T, :] * factor[c:c + 1, :]).astype(BF))
        share = jnp.concatenate(shares, axis=0)
        sg[j] = share
        term = nn(share, img_half[...])
        if o == 0:
            own_term[...] = term
        else:
            terms[o] = term.astype(BF)
            term_x.start(o, terms.at[o])

    texts = text_all[...].reshape(N * rows_t, W)
    for i in range(L):
        rows = slice(i * PI, (i + 1) * PI)
        grad = nn(sg[:, :, rows].reshape(N * rows_t, PI).T, texts)
        img_back[rows, :] = back_unit(grad, img_unit[rows, :], img_inv[rows, :]).astype(BF)

    cores = []

    def core_copy(m):
        return pltpu.make_async_remote_copy(
            src_ref=core_out.at[m],
            dst_ref=core_in.at[m],
            send_sem=core_s.at[m],
            recv_sem=core_r.at[m],
            device_id=mate,
            device_id_type=MESH,
        )

    def weight_grad(m, features_t, back):
        step = max(256, r)
        for d in range(0, H * r, step):
            out = nn(features_t[1 - core, d:d + step, :], back[...]).astype(BF)
            core_out[m, d // r:(d + step) // r] = out.reshape(step // r, r, W)
        copy = core_copy(m)
        copy.start()
        cores.append(copy)
        for d in range(0, H * r, step):
            out = nn(features_t[core, d:d + step, :], back[...])
            wg[m, d // r:(d + step) // r] = out.reshape(step // r, r, W)

    planes = [
        Exchange(chip, H, on_plane, plane_in.at[m], plane_s.at[m], plane_r.at[m], line=False) for m in range(2)
    ]
    rings = [Exchange(me, N, on_neg, ring_in.at[m], ring_s.at[m], ring_r.at[m]) for m in range(2)]
    fulls = [Exchange(me, N, on_neg, full.at[m], full_s.at[m], full_r.at[m]) for m in range(2)]

    def plane_send(m):
        cores[m].wait_recv()
        for o in range(1, H):
            k = planes[m].peer(o)
            plane_out[m, o] = (wg[m, k] + core_in[m, k].astype(F32)).astype(BF)
            planes[m].start(o, plane_out.at[m, o])
        plane_own[m] = wg[m, chip] + core_in[m, chip].astype(F32)

    def ring_send(m):
        value = plane_own[m]
        for o in range(1, H):
            value = value + plane_in[m, planes[m].take(o)].astype(F32)
        if split:
            value = value.reshape(N, rr, W)
            part[m] = value
            part_out[m] = value.astype(BF)
            for o in range(1, N):
                rings[m].start(o, part_out.at[m, rings[m].peer(o)])
        else:
            ring_in[m, me] = value.astype(BF)
            for o in range(1, N):
                rings[m].start(o, ring_in.at[m, me])

    def full_send(m):
        if split:
            value = part[m, me]
            for o in range(1, N):
                value = value + ring_in[m, rings[m].take(o)].astype(F32)
            full[m, me] = value.astype(BF)
            for o in range(1, N):
                fulls[m].start(o, full.at[m, me])

    saves = []

    def save(i, source, target):
        copy = pltpu.make_async_copy(source, target, save_sem.at[i])
        copy.start()
        saves.append(copy)

    def result(m, out):
        if split:
            for o in range(1, N):
                fulls[m].take(o)
            grads[m] = full[m].astype(F32).reshape(r, W)
        else:
            for o in range(1, N):
                rings[m].take(o)
            grads[m] = jnp.sum(ring_in[m].astype(F32), axis=0)
        save(2 + m, grads.at[m], out)

    weight_grad(0, img_t, img_back)
    fi[0:PI, :] = nt(img_back[0:PI, :], wi[...]).astype(BF)
    plane_send(0)

    grad = own_term[...]
    for o in range(1, N):
        grad = grad + term_in[term_x.take(o)].astype(F32)
    txt_back[...] = back_unit(grad, txt_unit[...], txt_inv[...]).astype(BF)
    weight_grad(1, txt_t, txt_back)
    ring_send(0)
    plane_send(1)
    ft[...] = nt(txt_back[...], wt[...]).astype(BF)
    save(1, ft, ft_hbm)
    for i in range(1, L):
        rows = slice(i * PI, (i + 1) * PI)
        fi[rows, :] = nt(img_back[rows, :], wi[...]).astype(BF)
    save(0, fi, fi_hbm)
    full_send(0)
    ring_send(1)
    result(0, gi_hbm)
    full_send(1)
    result(1, gt_hbm)

    for copy in cores:
        copy.wait_send()
    for copy in saves:
        copy.wait()
    for exchange in [text_x, term_x] + planes + rings + fulls:
        exchange.finish()


def write_out(*refs):
    sources, targets, held, in_sem, out_sem = refs[:4], refs[4:8], refs[8:12], refs[12], refs[13]
    loads, saves = [], []
    for source, target, hold in zip(sources, targets, held):
        rows = source.shape[0]
        step = rows // 4 if rows % 64 == 0 and source.dtype == BF else rows
        for at in range(0, rows, step):
            piece, i = pl.ds(at, step), len(loads)
            loads.append(pltpu.make_async_copy(source.at[piece], hold.at[piece], in_sem.at[i]))
            saves.append(pltpu.make_async_copy(hold.at[piece], target.at[piece], out_sem.at[i]))
    for load in loads:
        load.start()
    for load, save in zip(loads, saves):
        load.wait()
        save.start()
    for save in saves:
        save.wait()


def shards(n_dp, n_neg, img_features, txt_features, w_img, w_txt, cap_len, pairs):
    L, PI, D = img_features.shape
    T = txt_features.shape[1]
    W = w_img.shape[1]
    N, H, r = n_neg, n_dp // 2, D // n_dp
    rows_i, rows_t = L * PI, L * T
    rr = r // N if r % (16 * N) == 0 else r
    vmem, dma = pltpu.VMEM, pltpu.SemaphoreType.DMA
    scratch = [
        vmem((rows_i, D), BF), vmem((rows_t, D), BF), vmem((D, W), BF), vmem((D, W), BF),
        vmem((2, H * r, rows_i), BF), vmem((2, H * r, rows_t), BF),
        vmem((rows_i, W), F32), vmem((rows_i, 1), F32), vmem((rows_i, W), BF),
        vmem((rows_t, W), F32), vmem((rows_t, 1), F32),
        vmem((N, rows_t, W), BF), vmem((N, rows_t, rows_i), F32), vmem((N, 8, rows_i), F32),
        vmem((N, 8, 128), F32), vmem((N, rows_t, rows_i), BF),
        vmem((N, rows_t, W), BF), vmem((rows_t, W), F32), vmem((N, rows_t, W), BF),
        vmem((rows_i, W), BF), vmem((rows_t, W), BF),
        vmem((2, H, r, W), F32), vmem((2, H, r, W), BF), vmem((2, H, r, W), BF),
        vmem((2, H, r, W), BF), vmem((2, r, W), F32), vmem((2, H, r, W), BF),
        vmem((2, N, rr, W), F32), vmem((2, N, rr, W), BF),
        vmem((2, N, rr, W), BF), vmem((2, N, rr, W), BF),
        vmem((rows_i, D), BF), vmem((rows_t, D), BF), vmem((2, r, W), F32),
        dma((4,)), dma((4,)),
        dma((N,)), dma((N,)), dma((N,)), dma((N,)), dma((N,)), dma((N,)),
        dma((2,)), dma((2,)), dma((2, H)), dma((2, H)),
        dma((2, N)), dma((2, N)), dma((2, N)), dma((2, N)),
    ]
    shapes = (
        jax.ShapeDtypeStruct((rows_i, D), BF),
        jax.ShapeDtypeStruct((rows_t, D), BF),
        jax.ShapeDtypeStruct((r, W), F32),
        jax.ShapeDtypeStruct((r, W), F32),
    )
    results = pl.pallas_call(
        functools.partial(kernel, (L, PI, T, D, W, N, n_dp)),
        out_shape=shapes,
        in_specs=[pl.BlockSpec(memory_space=pltpu.HBM)] * 4
        + [pl.BlockSpec(memory_space=pltpu.SMEM)] * 2,
        out_specs=(pl.BlockSpec(memory_space=pltpu.HBM),) * 4,
        scratch_shapes=scratch,
        compiler_params=pltpu.CompilerParams(
            collective_id=0, has_side_effects=True, vmem_limit_bytes=VMEM_BYTES
        ),
    )(
        img_features.reshape(rows_i, D),
        txt_features.reshape(rows_t, D),
        w_img,
        w_txt,
        cap_len,
        pairs,
    )
    feat_img, feat_txt, final_img, final_txt = pl.pallas_call(
        write_out,
        out_shape=shapes,
        in_specs=[pl.BlockSpec(memory_space=pl.ANY)] * 4,
        out_specs=(pl.BlockSpec(memory_space=pltpu.HBM),) * 4,
        scratch_shapes=[vmem(shape.shape, shape.dtype) for shape in shapes]
        + [dma((16,)), dma((16,))],
        compiler_params=pltpu.CompilerParams(vmem_limit_bytes=VMEM_BYTES),
    )(*results)
    return (
        feat_img.reshape(img_features.shape),
        feat_txt.reshape(txt_features.shape),
        final_img,
        final_txt,
    )


def solution(mesh):
    in_specs = (
        P(("dp", "neg"), None, None),
        P(("dp", "neg"), None, None),
        P(),
        P(),
        P(("dp", "neg")),
        P("dp", None),
    )
    out_specs = (
        P(("dp", "neg"), None, None),
        P(("dp", "neg"), None, None),
        P("dp", None),
        P("dp", None),
    )
    body = functools.partial(shards, mesh.shape["dp"], mesh.shape["neg"])
    return jax.shard_map(body, mesh=mesh, in_specs=in_specs, out_specs=out_specs, check_vma=False)
```

```python
import functools

import jax
import jax.numpy as jnp
from jax import lax
from jax.experimental import pallas as pl
from jax.experimental.pallas import tpu as pltpu
from jax.sharding import PartitionSpec as P

TOKEN_SCALE = 100.0
PAIR_SCALE = 50.0
EPSILON = 1e-06
MARK = 4.0
LOW = -1e30
VMEM_BYTES = 60 * 1024 * 1024
BF = jnp.bfloat16
F32 = jnp.float32
MESH = pl.DeviceIdType.MESH


def nn(a, b):
    return lax.dot_general(a, b, (((1,), (0,)), ((), ())), preferred_element_type=F32)


def nt(a, b):
    return lax.dot_general(a, b, (((1,), (1,)), ((), ())), preferred_element_type=F32)


def unit_rows(projected):
    inverse = lax.rsqrt(jnp.sum(projected * projected, axis=-1, keepdims=True) + EPSILON)
    return projected * inverse, inverse


def back_unit(gradient, unit, inverse):
    return (gradient - unit * jnp.sum(unit * gradient, axis=-1, keepdims=True)) * inverse


class Exchange:
    def __init__(self, me, n, device, slots, send, recv, line=True):
        self.me, self.n, self.device, self.line = me, n, device, line
        self.slots, self.send, self.recv = slots, send, recv
        self.started = []

    def peer(self, offset):
        if not self.line:
            return lax.rem(self.me + offset, self.n)
        upper = lax.div(self.me * 2, self.n)
        k = upper * (offset - 1) + (1 - upper) * (self.n - 1 - offset)
        return k + lax.div(k + self.n - self.me, self.n)

    def start(self, offset, source):
        copy = pltpu.make_async_remote_copy(
            src_ref=source,
            dst_ref=self.slots.at[self.me],
            send_sem=self.send.at[offset],
            recv_sem=self.recv.at[self.me],
            device_id=self.device(self.peer(offset)),
            device_id_type=MESH,
        )
        copy.start()
        self.started.append(copy)

    def take(self, offset):
        other = self.peer(offset)
        pltpu.make_async_remote_copy(
            src_ref=self.slots.at[other],
            dst_ref=self.slots.at[other],
            send_sem=self.send.at[offset],
            recv_sem=self.recv.at[other],
            device_id=self.device(other),
            device_id_type=MESH,
        ).wait_recv()
        return other

    def finish(self):
        for copy in self.started:
            copy.wait_send()


def kernel(
    dims,
    img_hbm, txt_hbm, wi_hbm, wt_hbm, cap, pairs,
    fi_hbm, ft_hbm, gi_hbm, gt_hbm,
    img, txt, wi, wt, img_t, txt_t,
    img_unit, img_inv, img_half, txt_unit, txt_inv,
    text_all, expo, total, logit_all, sg, terms, own_term, term_in,
    img_back, txt_back, wg, core_out, core_in, plane_out, plane_own, plane_in,
    part, part_out, ring_in, wide_in, full, fi, ft, grads,
    load_sem, save_sem,
    text_s, text_r, logit_s, logit_r, term_s, term_r,
    core_s, core_r, plane_s, plane_r, ring_s, ring_r, full_s, full_r,
):
    L, PI, T, D, W, N, NDP = dims
    H = NDP // 2
    r = D // NDP
    rows_i, rows_t = L * PI, L * T
    dp = lax.axis_index("dp")
    me = lax.axis_index("neg")
    core = lax.rem(dp, 2)
    chip = lax.div(dp, 2)
    split = r % (16 * N) == 0
    rr = r // N if split else r

    loads = [
        pltpu.make_async_copy(source, target, load_sem.at[i])
        for i, (source, target) in enumerate(
            ((txt_hbm, txt), (wt_hbm, wt), (wi_hbm, wi), (img_hbm, img))
        )
    ]
    for load in loads:
        load.start()

    def on_neg(k):
        return (dp, k)

    def on_plane(k):
        return (k * 2 + core, me)

    barrier = pltpu.get_barrier_semaphore()
    for o in range(1, N):
        pl.semaphore_signal(barrier, inc=1, device_id=on_neg(lax.rem(me + o, N)), device_id_type=MESH)
    for o in range(1, H):
        pl.semaphore_signal(
            barrier, inc=1, device_id=on_plane(lax.rem(chip + o, H)), device_id_type=MESH
        )
    mate = (chip * 2 + 1 - core, me)
    pl.semaphore_signal(barrier, inc=1, device_id=mate, device_id_type=MESH)

    loads[0].wait()
    loads[1].wait()
    unit, inverse = unit_rows(nn(txt[...], wt[...]))
    txt_unit[...] = unit
    txt_inv[...] = inverse
    place = lax.broadcasted_iota(jnp.int32, (T, W), 0)
    for c in range(L):
        text_all[me, c * T:(c + 1) * T, :] = jnp.where(
            place < cap[c], unit[c * T:(c + 1) * T], MARK
        ).astype(BF)
    pl.semaphore_wait(barrier, N - 1 + H - 1 + 1)
    text_x = Exchange(me, N, on_neg, text_all, text_s, text_r)
    for o in range(1, N):
        text_x.start(o, text_all.at[me])

    loads[2].wait()
    loads[3].wait()
    for i in range(L):
        rows = slice(i * PI, (i + 1) * PI)
        unit, inverse = unit_rows(nn(img[rows, :], wi[...]))
        img_unit[rows, :] = unit
        img_inv[rows, :] = inverse
        img_half[rows, :] = unit.astype(BF)

    def transpose_features(features, features_t, start, size):
        step = max(256, r)
        for d in range(0, D, step):
            turned = features[start:start + size, d:d + step].T
            for k in range(d // r, (d + step) // r):
                at = k // 2 * r
                features_t[k % 2, at:at + r, start:start + size] = turned[k * r - d:(k + 1) * r - d]

    lane = lax.broadcasted_iota(jnp.int32, (8, 128), 1)
    line = lax.broadcasted_iota(jnp.int32, (8, 128), 0)

    def pool(j, tile):
        text = text_all[j]
        marks = text[:, 0:128].astype(F32)
        marks = jnp.concatenate([marks] * (rows_i // 128), axis=1)
        scores = jnp.where(marks < 2.0, TOKEN_SCALE * nt(text, img_half[...]), LOW)
        scores = scores.reshape(L, T, rows_i)
        peaks = jnp.max(scores, axis=1, keepdims=True)
        expos = jnp.exp(scores - peaks)
        totals = jnp.sum(expos, axis=1)
        expo[j] = expos.reshape(rows_t, rows_i)
        total[j] = jnp.concatenate([totals, jnp.ones((8 - L, rows_i), F32)], axis=0)
        pooled = peaks[:, 0, :] + jnp.log(totals)
        pooled = jnp.concatenate([pooled, jnp.zeros((8 - L, rows_i), F32)], axis=0)
        for i in range(L):
            mean = jnp.sum(pooled[:, i * PI:(i + 1) * PI], axis=1, keepdims=True)
            mean = mean * (PAIR_SCALE / (TOKEN_SCALE * PI))
            tile = jnp.where((lane == j * L + i) & (line < L), mean, tile)
        return tile

    tile = pool(me, jnp.full((8, 128), LOW, F32))
    for i in range(L):
        transpose_features(img, img_t, i * PI, PI)
    for o in reversed(range(1, N)):
        tile = pool(text_x.take(o), tile)
    logit_all[me] = tile
    logit_x = Exchange(me, N, on_neg, logit_all, logit_s, logit_r)
    for o in range(1, N):
        logit_x.start(o, logit_all.at[me])
    transpose_features(txt, txt_t, 0, rows_t)
    owner, image = lax.div(lane, L), lax.rem(lane, L)

    def over_images(value, reduce, fill):
        out = value
        for j in range(N):
            mine = owner == j
            total = reduce(jnp.where(mine, value, fill), axis=1, keepdims=True)
            out = jnp.where(mine, total, out)
        return out

    row_prob = jnp.zeros((8, 128), F32)
    target = jnp.zeros((8, 128), F32)
    for i in range(L):
        mine = image == i
        values = jnp.where(mine, tile, LOW)
        row_top = jnp.max(jnp.max(values, axis=1, keepdims=True), axis=0, keepdims=True)
        row_exp = jnp.exp(values - row_top)
        row_sum = jnp.sum(jnp.sum(row_exp, axis=1, keepdims=True), axis=0, keepdims=True)
        row_prob = jnp.where(mine, row_exp / row_sum, row_prob)
        hit = mine & (owner * L + line == pairs[0, me * L + i])
        target = jnp.where(hit, 1.0, target)
    for o in range(1, N):
        logit_x.take(o)
    everyone = logit_all[...]
    col_top = over_images(jnp.max(everyone, axis=0), jnp.max, LOW)
    col_sum = over_images(jnp.sum(jnp.exp(everyone - col_top[None]), axis=0), jnp.sum, 0.0)
    col_prob = jnp.exp(tile - col_top) / col_sum
    pair_grad = (row_prob + col_prob - 2.0 * target) * (PAIR_SCALE / (2.0 * N * L * PI))
    logit_x.finish()

    term_x = Exchange(me, N, on_neg, term_in, term_s, term_r)
    for o in list(range(1, N)) + [0]:
        j = term_x.peer(o) if o else me
        spread = jnp.concatenate(
            [
                jnp.broadcast_to(
                    jnp.sum(jnp.where(lane == j * L + i, pair_grad, 0.0), axis=1, keepdims=True),
                    (8, PI),
                )
                for i in range(L)
            ],
            axis=1,
        )
        factor = spread / total[j]
        shares = []
        for c in range(L):
            shares.append((expo[j, c * T:(c + 1) * T, :] * factor[c:c + 1, :]).astype(BF))
        share = jnp.concatenate(shares, axis=0)
        sg[j] = share
        term = nn(share, img_half[...])
        if o == 0:
            own_term[...] = term
        else:
            terms[o] = term.astype(BF)
            term_x.start(o, terms.at[o])

    texts = text_all[...].reshape(N * rows_t, W)
    for i in range(L):
        rows = slice(i * PI, (i + 1) * PI)
        grad = nn(sg[:, :, rows].reshape(N * rows_t, PI).T, texts)
        img_back[rows, :] = back_unit(grad, img_unit[rows, :], img_inv[rows, :]).astype(BF)

    cores = []

    def core_copy(m):
        return pltpu.make_async_remote_copy(
            src_ref=core_out.at[m],
            dst_ref=core_in.at[m],
            send_sem=core_s.at[m],
            recv_sem=core_r.at[m],
            device_id=mate,
            device_id_type=MESH,
        )

    def weight_grad(m, features_t, back):
        step = max(256, r)
        for d in range(0, H * r, step):
            out = nn(features_t[1 - core, d:d + step, :], back[...]).astype(BF)
            core_out[m, d // r:(d + step) // r] = out.reshape(step // r, r, W)
        copy = core_copy(m)
        copy.start()
        cores.append(copy)
        for d in range(0, H * r, step):
            out = nn(features_t[core, d:d + step, :], back[...])
            wg[m, d // r:(d + step) // r] = out.reshape(step // r, r, W)

    planes = [
        Exchange(chip, H, on_plane, plane_in.at[m], plane_s.at[m], plane_r.at[m], line=False) for m in range(2)
    ]
    splits = (split, False)
    slots = (ring_in if split else wide_in.at[0], wide_in.at[1])
    rings = [Exchange(me, N, on_neg, slots[m], ring_s.at[m], ring_r.at[m]) for m in range(2)]
    fulls = [Exchange(me, N, on_neg, full.at[m], full_s.at[m], full_r.at[m]) for m in range(2)]

    def plane_send(m):
        cores[m].wait_recv()
        for o in range(1, H):
            k = planes[m].peer(o)
            plane_out[m, o] = (wg[m, k] + core_in[m, k].astype(F32)).astype(BF)
            planes[m].start(o, plane_out.at[m, o])
        plane_own[m] = wg[m, chip] + core_in[m, chip].astype(F32)

    def ring_send(m):
        value = plane_own[m]
        for o in range(1, H):
            value = value + plane_in[m, planes[m].take(o)].astype(F32)
        if splits[m]:
            value = value.reshape(N, rr, W)
            part[m] = value
            part_out[m] = value.astype(BF)
            for o in range(1, N):
                rings[m].start(o, part_out.at[m, rings[m].peer(o)])
        else:
            wide_in[m, me] = value.astype(BF)
            for o in range(1, N):
                rings[m].start(o, wide_in.at[m, me])

    def full_send(m):
        if splits[m]:
            value = part[m, me]
            for o in range(1, N):
                value = value + ring_in[rings[m].take(o)].astype(F32)
            full[m, me] = value.astype(BF)
            for o in range(1, N):
                fulls[m].start(o, full.at[m, me])

    saves = []

    def save(i, source, target):
        copy = pltpu.make_async_copy(source, target, save_sem.at[i])
        copy.start()
        saves.append(copy)

    def result(m, out):
        if splits[m]:
            for o in range(1, N):
                fulls[m].take(o)
            grads[m] = full[m].astype(F32).reshape(r, W)
        else:
            for o in range(1, N):
                rings[m].take(o)
            grads[m] = jnp.sum(wide_in[m].astype(F32), axis=0)
        save(2 + m, grads.at[m], out)

    weight_grad(0, img_t, img_back)
    fi[0:PI, :] = nt(img_back[0:PI, :], wi[...]).astype(BF)
    plane_send(0)

    grad = own_term[...]
    for o in range(1, N):
        grad = grad + term_in[term_x.take(o)].astype(F32)
    txt_back[...] = back_unit(grad, txt_unit[...], txt_inv[...]).astype(BF)
    weight_grad(1, txt_t, txt_back)
    ring_send(0)
    plane_send(1)
    ft[...] = nt(txt_back[...], wt[...]).astype(BF)
    save(1, ft, ft_hbm)
    for i in range(1, L):
        rows = slice(i * PI, (i + 1) * PI)
        fi[rows, :] = nt(img_back[rows, :], wi[...]).astype(BF)
    save(0, fi, fi_hbm)
    full_send(0)
    ring_send(1)
    result(0, gi_hbm)
    full_send(1)
    result(1, gt_hbm)

    for copy in cores:
        copy.wait_send()
    for copy in saves:
        copy.wait()
    for exchange in [text_x, term_x] + planes + rings + fulls:
        exchange.finish()


def write_out(*refs):
    sources, targets, held, in_sem, out_sem = refs[:4], refs[4:8], refs[8:12], refs[12], refs[13]
    loads, saves = [], []
    for source, target, hold in zip(sources, targets, held):
        rows = source.shape[0]
        step = rows // 4 if rows % 64 == 0 and source.dtype == BF else rows
        for at in range(0, rows, step):
            piece, i = pl.ds(at, step), len(loads)
            loads.append(pltpu.make_async_copy(source.at[piece], hold.at[piece], in_sem.at[i]))
            saves.append(pltpu.make_async_copy(hold.at[piece], target.at[piece], out_sem.at[i]))
    for load in loads:
        load.start()
    for load, save in zip(loads, saves):
        load.wait()
        save.start()
    for save in saves:
        save.wait()


def shards(n_dp, n_neg, img_features, txt_features, w_img, w_txt, cap_len, pairs):
    L, PI, D = img_features.shape
    T = txt_features.shape[1]
    W = w_img.shape[1]
    N, H, r = n_neg, n_dp // 2, D // n_dp
    rows_i, rows_t = L * PI, L * T
    rr = r // N if r % (16 * N) == 0 else r
    vmem, dma = pltpu.VMEM, pltpu.SemaphoreType.DMA
    scratch = [
        vmem((rows_i, D), BF), vmem((rows_t, D), BF), vmem((D, W), BF), vmem((D, W), BF),
        vmem((2, H * r, rows_i), BF), vmem((2, H * r, rows_t), BF),
        vmem((rows_i, W), F32), vmem((rows_i, 1), F32), vmem((rows_i, W), BF),
        vmem((rows_t, W), F32), vmem((rows_t, 1), F32),
        vmem((N, rows_t, W), BF), vmem((N, rows_t, rows_i), F32), vmem((N, 8, rows_i), F32),
        vmem((N, 8, 128), F32), vmem((N, rows_t, rows_i), BF),
        vmem((N, rows_t, W), BF), vmem((rows_t, W), F32), vmem((N, rows_t, W), BF),
        vmem((rows_i, W), BF), vmem((rows_t, W), BF),
        vmem((2, H, r, W), F32), vmem((2, H, r, W), BF), vmem((2, H, r, W), BF),
        vmem((2, H, r, W), BF), vmem((2, r, W), F32), vmem((2, H, r, W), BF),
        vmem((2, N, rr, W), F32), vmem((2, N, rr, W), BF),
        vmem((N, rr, W), BF), vmem((2, N, r, W), BF), vmem((2, N, rr, W), BF),
        vmem((rows_i, D), BF), vmem((rows_t, D), BF), vmem((2, r, W), F32),
        dma((4,)), dma((4,)),
        dma((N,)), dma((N,)), dma((N,)), dma((N,)), dma((N,)), dma((N,)),
        dma((2,)), dma((2,)), dma((2, H)), dma((2, H)),
        dma((2, N)), dma((2, N)), dma((2, N)), dma((2, N)),
    ]
    shapes = (
        jax.ShapeDtypeStruct((rows_i, D), BF),
        jax.ShapeDtypeStruct((rows_t, D), BF),
        jax.ShapeDtypeStruct((r, W), F32),
        jax.ShapeDtypeStruct((r, W), F32),
    )
    results = pl.pallas_call(
        functools.partial(kernel, (L, PI, T, D, W, N, n_dp)),
        out_shape=shapes,
        in_specs=[pl.BlockSpec(memory_space=pltpu.HBM)] * 4
        + [pl.BlockSpec(memory_space=pltpu.SMEM)] * 2,
        out_specs=(pl.BlockSpec(memory_space=pltpu.HBM),) * 4,
        scratch_shapes=scratch,
        compiler_params=pltpu.CompilerParams(
            collective_id=0, has_side_effects=True, vmem_limit_bytes=VMEM_BYTES
        ),
    )(
        img_features.reshape(rows_i, D),
        txt_features.reshape(rows_t, D),
        w_img,
        w_txt,
        cap_len,
        pairs,
    )
    feat_img, feat_txt, final_img, final_txt = pl.pallas_call(
        write_out,
        out_shape=shapes,
        in_specs=[pl.BlockSpec(memory_space=pl.ANY)] * 4,
        out_specs=(pl.BlockSpec(memory_space=pltpu.HBM),) * 4,
        scratch_shapes=[vmem(shape.shape, shape.dtype) for shape in shapes]
        + [dma((16,)), dma((16,))],
        compiler_params=pltpu.CompilerParams(vmem_limit_bytes=VMEM_BYTES),
    )(*results)
    return (
        feat_img.reshape(img_features.shape),
        feat_txt.reshape(txt_features.shape),
        final_img,
        final_txt,
    )


def solution(mesh):
    in_specs = (
        P(("dp", "neg"), None, None),
        P(("dp", "neg"), None, None),
        P(),
        P(),
        P(("dp", "neg")),
        P("dp", None),
    )
    out_specs = (
        P(("dp", "neg"), None, None),
        P(("dp", "neg"), None, None),
        P("dp", None),
        P("dp", None),
    )
    body = functools.partial(shards, mesh.shape["dp"], mesh.shape["neg"])
    return jax.shard_map(body, mesh=mesh, in_specs=in_specs, out_specs=out_specs, check_vma=False)
```
